32 devices in a mesh: pair: 8 (over y, x, core), ph: 4 (over z).
Axes of the slice: x: 2, y: 2, z: 4, core: 2. Of those that a mesh axis runs over, the one named last changes fastest.
Arguments:
- t_cycle: float32 [8, 512, 8192], P(None, 'pair', 'ph'), may hold values from -6 to 6
- w_cycle: float32 [8, 8192, 4096], P(None, 'ph', 'pair'), may hold values from -0.1875 to 0.1875
- occ_energy: float32 [64], replicated, may hold values from -1.5 to -0.5
- vir_energy: float32 [8, 128], replicated, may hold values from 0.2 to 1.5
- occ_irrep: int32 [64], replicated, may hold values from 0 to 7
- vir_count: int32 [8], replicated, may hold values from 1 to 128, 640 in all
Outputs:
- increment: float32 [8, 512, 4096], P(None, 'ph', 'pair')
The draws below stay inside these ranges and needn't reach their ends.
Inputs may be any that keep to these rules, and one draw needn't show every extreme that they name: `occ_irrep`: irrep labels combine by exclusive or. `vir_count`: the counts sum to 640; one irrep fills all 128 slots.
All inputs are finite; a program needn't handle non-finite values.
Results may differ from the reference program's by a relative error of at most 0.000075.
Values sent between devices are 32-bit elements; how exact they have to be, the bound alone decides.
A program may use at most 128 MiB of HBM per device.

```python
import math
import jax
import jax.numpy as jnp
import numpy as np
from jax import lax

IRREPS = 8
OCCUPIED = 64
VIRT_CAP = 128
VIRTUALS = 640
ROW_OCC = 4
COL_OCC = 32
ROWS = 512
PAIRS = 8192
COLS = 4096


def set_ends(result, own_key, low, top_value):
    spot = [jax.random.randint(jax.random.fold_in(own_key, axis), (), 0, length) for axis, length in enumerate(result.shape)]
    widest = result.shape.index(max(result.shape))
    neighbour = spot[:widest] + [(spot[widest] + 1) % result.shape[widest]] + spot[widest + 1:]
    return result.at[tuple(spot)].set(low).at[tuple(neighbour)].set(top_value)


def steps_of(rng, dims, cuts, smallest, high):
    factor_of = 1.0
    for dim, parts in cuts:
        draws = jax.random.uniform(jax.random.fold_in(jax.random.fold_in(rng, 6), dim), (parts,), jnp.float32, smallest / len(cuts), high / len(cuts))
        factor_of = factor_of * jnp.repeat(jnp.exp(draws), dims[dim] // parts).reshape((-1,) + (1,) * (len(dims) - 1 - dim))
    return factor_of


def profile(amount, total, bound, skew):
    portions = [(1 << 20) // math.isqrt(grade ** skew) + 1 for grade in range(2, amount + 1)]
    rest, given = total - bound - (amount - 1), [1] * (amount - 1)
    while rest > 0:
        movable = [i for i in range(amount - 1) if given[i] < bound]
        mass, left = sum([portions[i] for i in movable]), rest
        for i in movable:
            more = min(bound - given[i], max(1, left * portions[i] // mass), rest)
            given[i] = given[i] + more
            rest = rest - more
    return np.array([bound] + given)


def ragged_sizes(rng, amount, total, bound, lean):
    if amount == 2:
        one = jax.random.randint(rng, (), max(1, total - bound), min(bound, total - 1) + 1)
        return jnp.stack([one, total - one])
    sizes = jnp.asarray(profile(amount, total, bound, lean), jnp.int32)
    pairs = (amount - 1) // 2
    giver, receiver = sizes[1:1 + 2 * pairs:2], sizes[2:2 + 2 * pairs:2]
    margin = jnp.minimum(giver - 1, bound - receiver)
    passed = jax.random.randint(jax.random.fold_in(rng, 1), (pairs,), 0, 1 << 20) % (margin + 1)
    sizes = sizes.at[1:1 + 2 * pairs:2].set(giver - passed).at[2:2 + 2 * pairs:2].set(receiver + passed)
    return sizes[jax.random.permutation(jax.random.fold_in(rng, 2), amount)]


def bell_draw(own_key, shape, width, most, shards=(), kind=jnp.bfloat16):
    array = jax.random.normal(own_key, shape, jnp.float32) * width
    if len(shards) > 0:
        array = steps_of(own_key, shape, shards, -0.22, 0.18) * array
    return jnp.clip(array, min=-most, max=most).astype(kind)


def setup_inputs(seed: int = 0) -> dict:
    splits = jax.random.split(jax.random.key(seed), 7)
    t_cycle = bell_draw(splits[0], (IRREPS, ROWS, PAIRS), 1.0, 6.0, ((1, 8), (2, 4)), jnp.float32)
    w_cycle = bell_draw(splits[1], (IRREPS, PAIRS, COLS), (PAIRS // IRREPS) ** -0.5, 0.1875, ((1, 4), (2, 8)), jnp.float32)
    occ_energy = jnp.clip(jax.random.uniform(splits[2], (OCCUPIED,), jnp.float32, -1.5, -0.5), -1.5, -0.5)
    vir_energy = jnp.clip(jax.random.uniform(splits[3], (IRREPS, VIRT_CAP), jnp.float32, 0.2, 1.5), 0.2, 1.5)
    occ_irrep = set_ends(jax.random.randint(splits[4], (OCCUPIED,), 0, IRREPS), jax.random.fold_in(splits[4], 1), 0, IRREPS - 1).astype(jnp.int32)
    vir_count = ragged_sizes(splits[5], IRREPS, VIRTUALS, VIRT_CAP, 1).astype(jnp.int32)
    return dict(t_cycle=t_cycle, w_cycle=w_cycle, occ_energy=occ_energy, vir_energy=vir_energy, occ_irrep=occ_irrep, vir_count=vir_count)


def reference(t_cycle, w_cycle, occ_energy, vir_energy, occ_irrep, vir_count):
    slot_ids = jnp.arange(VIRT_CAP, dtype=jnp.int32)
    irreps = jnp.arange(IRREPS, dtype=jnp.int32)
    symmetry = jnp.bitwise_xor(occ_irrep[None, :], irreps[:, None]).astype(jnp.int32)
    counts = vir_count[symmetry]
    live_slot = (slot_ids[None, None, :] < counts[:, :, None]).astype(jnp.float32)
    vir_ener = vir_energy[symmetry]
    mask_pair = live_slot.reshape(IRREPS, PAIRS)
    mask_row = live_slot[:, :ROW_OCC].reshape(IRREPS, ROWS)
    mask_col = live_slot[:, :COL_OCC].reshape(IRREPS, COLS)
    e_row = (occ_energy[None, :ROW_OCC, None] - vir_ener[:, :ROW_OCC]).reshape(IRREPS, ROWS)
    e_col = (occ_energy[None, :COL_OCC, None] - vir_ener[:, :COL_OCC]).reshape(IRREPS, COLS)

    def contract(irrep):
        masked = w_cycle[irrep] * mask_pair[irrep][:, None]
        return jnp.dot(t_cycle[irrep], masked, precision=lax.Precision.HIGHEST, preferred_element_type=jnp.float32)

    cycle = lax.map(contract, irreps)
    return mask_row[:, :, None] * mask_col[:, None, :] * cycle / (e_row[:, :, None] + e_col[:, None, :])
```

```python
import jax
import jax.numpy as jnp
from jax import lax
from jax.sharding import PartitionSpec as P

IRREPS = 8
VIRT_CAP = 128
ROW_OCC = 4
COL_OCC = 32
ROWS = 512
PAIRS = 8192
COLS = 4096


def reduce_rows(partial_value):
    return lax.psum_scatter(partial_value, "ph", scatter_dimension=1, tiled=True)


def on_device(t_cycle, w_cycle, occ_energy, vir_energy, occ_irrep, vir_count):
    n_pair = lax.axis_size("pair")
    n_ph = lax.axis_size("ph")
    ph_index = lax.axis_index("ph")
    pair_index = lax.axis_index("pair")
    local_rows = t_cycle.shape[1]
    local_pairs = t_cycle.shape[2]
    local_cols = w_cycle.shape[2]
    out_rows = local_rows * n_pair // n_ph
    slot_ids = jnp.arange(VIRT_CAP, dtype=jnp.int32)
    irreps = jnp.arange(IRREPS, dtype=jnp.int32)
    symmetry = jnp.bitwise_xor(occ_irrep[None, :], irreps[:, None])
    onehot = symmetry[:, :, None] == irreps[None, None, :]
    counts = jnp.sum(jnp.where(onehot, vir_count[None, None, :], 0), axis=2)
    live_slot = (slot_ids[None, None, :] < counts[:, :, None]).astype(jnp.float32)
    vir_ener = jnp.einsum(
        "goh,hv->gov",
        onehot.astype(jnp.float32),
        vir_energy,
        precision=lax.Precision.HIGHEST,
        preferred_element_type=jnp.float32,
    )
    mask_pair = lax.dynamic_slice_in_dim(
        live_slot.reshape(IRREPS, PAIRS), ph_index * local_pairs, local_pairs, 1
    )
    mask_row = lax.dynamic_slice_in_dim(
        live_slot[:, :ROW_OCC].reshape(IRREPS, ROWS), ph_index * out_rows, out_rows, 1
    )
    mask_col = lax.dynamic_slice_in_dim(
        live_slot[:, :COL_OCC].reshape(IRREPS, COLS), pair_index * local_cols, local_cols, 1
    )
    e_row = (occ_energy[None, :ROW_OCC, None] - vir_ener[:, :ROW_OCC]).reshape(IRREPS, ROWS)
    e_col = (occ_energy[None, :COL_OCC, None] - vir_ener[:, :COL_OCC]).reshape(IRREPS, COLS)
    e_row = lax.dynamic_slice_in_dim(e_row, ph_index * out_rows, out_rows, 1)
    e_col = lax.dynamic_slice_in_dim(e_col, pair_index * local_cols, local_cols, 1)
    step = max(1, IRREPS // 4)
    gathered = [
        lax.all_gather(t_cycle[first : first + step], "pair", axis=1, tiled=True)
        for first in range(0, IRREPS, step)
    ]
    pieces = []
    for first, rows in zip(range(0, IRREPS, step), gathered):
        partial_value = jnp.einsum(
            "grk,gkc->grc",
            rows,
            w_cycle[first : first + step] * mask_pair[first : first + step, :, None],
            precision=lax.Precision.HIGH,
            preferred_element_type=jnp.float32,
        )
        pieces.append(reduce_rows(partial_value))
    summed = jnp.concatenate(pieces, axis=0)
    return (
        mask_row[:, :, None]
        * mask_col[:, None, :]
        * summed
        / (e_row[:, :, None] + e_col[:, None, :])
    )


def solution(mesh):
    return jax.shard_map(
        on_device,
        mesh=mesh,
        in_specs=(P(None, "pair", "ph"), P(None, "ph", "pair"), P(), P(), P(), P()),
        out_specs=P(None, "ph", "pair"),
        check_vma=False,
    )
```

```python
import functools

import jax
import jax.numpy as jnp
from jax import lax
from jax.experimental import pallas as pl
from jax.experimental.pallas import tpu as pltpu
from jax.sharding import PartitionSpec as P

IRREPS = 8
VIRT_CAP = 128
VIRTUALS = 640
ROW_OCC = 4
CHUNKS = 5
VMEM_LIMIT = 56 * 1024 * 1024


def offsets_of(count_ref):
    offs = [jnp.int32(0)]
    for h in range(IRREPS):
        offs.append(offs[-1] + count_ref[h])
    return offs


def pick(values, index):
    result = values[0]
    for position in range(1, len(values)):
        result = jnp.where(index == position, values[position], result)
    return result


def split_kernel(irrep_ref, count_ref, w_ref, hi_ref, lo_ref):
    g = pl.program_id(0)
    tile = w_ref.shape[1]
    per_tile = tile // VIRT_CAP
    first = (lax.axis_index("ph") * pl.num_programs(1) + pl.program_id(1)) * per_tile
    slot = lax.broadcasted_iota(jnp.int32, (VIRT_CAP, w_ref.shape[2]), 0)
    for k in range(per_tile):
        live = slot < count_ref[jnp.bitwise_xor(irrep_ref[first + k], g)]
        rows = pl.ds(k * VIRT_CAP, VIRT_CAP)
        value = jnp.where(live, w_ref[0, rows, :], 0.0)
        high = value.astype(jnp.bfloat16)
        hi_ref[0, rows, :] = high
        lo_ref[0, rows, :] = (value - high.astype(jnp.float32)).astype(jnp.bfloat16)


def split_weights(occ_irrep, vir_count, w):
    irreps, pairs, cols = w.shape
    tile = min(pairs, 1024)
    spec = pl.BlockSpec((1, tile, cols), lambda g, p, *_: (g, p, 0))
    part = jax.ShapeDtypeStruct(w.shape, jnp.bfloat16)
    return pl.pallas_call(
        split_kernel,
        out_shape=(part, part),
        grid_spec=pltpu.PrefetchScalarGridSpec(
            num_scalar_prefetch=2, grid=(irreps, pairs // tile), in_specs=[spec], out_specs=[spec, spec]
        ),
        compiler_params=pltpu.CompilerParams(vmem_limit_bytes=VMEM_LIMIT),
        cost_estimate=pl.CostEstimate(flops=4 * w.size, bytes_accessed=8 * w.size, transcendentals=0),
    )(occ_irrep, vir_count, w)


def compact_kernel(group, irrep_ref, count_ref, *refs):
    parts, outs = refs[:group], refs[group:]
    me = lax.axis_index("pair")
    sub, i = lax.rem(me, group), lax.div(me, group)
    local = parts[0].shape[1]
    half = outs[0].shape[0]
    offs = offsets_of(count_ref)
    irrep = irrep_ref[i]
    for piece, out in enumerate(outs):
        start = (piece // 2) * (2 * half * group) + sub * (2 * half) + (piece % 2) * half

        @pl.loop(0, half, unroll=4)
        def _(r, out=out, start=start):
            v = start + r
            h, base = jnp.int32(0), jnp.int32(0)
            for m in range(1, IRREPS):
                past = offs[m] <= v
                h = jnp.where(past, m, h)
                base = jnp.where(past, offs[m], base)
            a = v - base
            g = jnp.bitwise_xor(irrep, h)
            owner, row = jnp.bitwise_xor(lax.div(a, local), sub), lax.rem(a, local)
            if group == 2:
                out[pl.ds(r, 1), :] = jnp.where(
                    owner == 0, parts[0][g, pl.ds(row, 1), :], parts[1][g, pl.ds(row, 1), :]
                )
            else:
                for m in range(group):

                    @pl.when(owner == m)
                    def _(m=m):
                        out[pl.ds(r, 1), :] = parts[m][g, pl.ds(row, 1), :]


def compact_rows(occ_irrep, vir_count, parts):
    group = len(parts)
    half = VIRTUALS // (CHUNKS * group * 2)
    pairs = parts[0].shape[2]
    vmem = pl.BlockSpec(memory_space=pltpu.VMEM)
    smem = pl.BlockSpec(memory_space=pltpu.SMEM)
    return pl.pallas_call(
        functools.partial(compact_kernel, group),
        out_shape=[jax.ShapeDtypeStruct((half, pairs), jnp.float32)] * (2 * CHUNKS),
        in_specs=[smem, smem] + [vmem] * group,
        out_specs=[vmem] * (2 * CHUNKS),
        compiler_params=pltpu.CompilerParams(vmem_limit_bytes=VMEM_LIMIT),
    )(occ_irrep, vir_count, *parts)


def product_kernel(group, chunk, irrep_ref, count_ref, *refs):
    n_parts = 2 * group * ROW_OCC
    parts, (whi_ref, wlo_ref, out_ref, rows_ref, both_ref) = refs[:n_parts], refs[n_parts:]
    i, h = pl.program_id(0), pl.program_id(1)
    me = lax.axis_index("pair")
    sub, mine = lax.rem(me, group), lax.div(me, group)
    half = parts[0].shape[0]
    rows = rows_ref.shape[0]

    @pl.when(h == 0)
    def _():
        for q in range(ROW_OCC):

            @pl.when(jnp.bitwise_xor(i, mine) == q)
            def _(q=q):
                for c in range(group):
                    at = jnp.bitwise_xor(sub, c) * (2 * half)
                    for side in range(2):
                        rows_ref[pl.ds(pl.multiple_of(at + side * half, 8), half), :] = parts[
                            (q * group + c) * 2 + side
                        ][...]

        value = rows_ref[...]
        high = value.astype(jnp.bfloat16)
        both_ref[:rows, :] = high
        both_ref[rows:, :] = (value - high.astype(jnp.float32)).astype(jnp.bfloat16)
        out_ref[...] = jnp.zeros_like(out_ref)

    offs = offsets_of(count_ref)
    low, top = pick(offs[:-1], h) - chunk * rows, pick(offs[1:], h) - chunk * rows

    @pl.when((low < rows) & (top > 0))
    def _():
        first = jnp.dot(both_ref[...], whi_ref[0], preferred_element_type=jnp.float32)
        second = jnp.dot(both_ref[:rows, :], wlo_ref[0], preferred_element_type=jnp.float32)
        total = first[:rows] + (first[rows:] + second)
        row = lax.broadcasted_iota(jnp.int32, total.shape, 0)
        out_ref[0] = jnp.where((row >= low) & (row < top), total, out_ref[0])


def product(occ_irrep, vir_count, chunk, parts, w_hi, w_lo, group):
    rows = VIRTUALS // CHUNKS
    irreps, pairs, cols = w_hi.shape

    def block_of(i, h, irrep_ref, count_ref):
        offs = offsets_of(count_ref)
        first, last = jnp.int32(0), jnp.int32(-1)
        for m in range(IRREPS):
            first = first + jnp.where(offs[m + 1] <= chunk * rows, 1, 0)
            last = last + jnp.where(offs[m] < (chunk + 1) * rows, 1, 0)
        return jnp.bitwise_xor(irrep_ref[i], jnp.clip(h, first, last)), 0, 0

    t_spec = pl.BlockSpec(parts[0].shape, lambda i, h, *_: (0, 0), pipeline_mode=pl.Buffered(1))
    w_spec = pl.BlockSpec((1, pairs, cols), block_of)
    out = pl.pallas_call(
        functools.partial(product_kernel, group, chunk),
        out_shape=jax.ShapeDtypeStruct((ROW_OCC, rows, cols), jnp.float32),
        grid_spec=pltpu.PrefetchScalarGridSpec(
            num_scalar_prefetch=2,
            grid=(ROW_OCC, irreps),
            in_specs=[t_spec] * len(parts) + [w_spec, w_spec],
            out_specs=pl.BlockSpec((1, rows, cols), lambda i, h, *_: (i, 0, 0)),
            scratch_shapes=[pltpu.VMEM((rows, pairs), jnp.float32), pltpu.VMEM((2 * rows, pairs), jnp.bfloat16)],
        ),
        compiler_params=pltpu.CompilerParams(vmem_limit_bytes=VMEM_LIMIT),
        cost_estimate=pl.CostEstimate(
            flops=2 * 6 * 2 * ROW_OCC * rows * pairs * cols, bytes_accessed=40 * 2**20, transcendentals=0
        ),
    )(occ_irrep, vir_count, *parts, w_hi, w_lo)
    return out.reshape(ROW_OCC * rows, cols)


def expand_kernel(share, irrep_ref, count_ref, occ_ref, vir_ref, vir_t_ref, *refs):
    pieces, (out_ref, all_ref) = refs[:CHUNKS], refs[CHUNKS:]
    g = pl.program_id(0)
    ph, pair = lax.axis_index("ph"), lax.axis_index("pair")
    rows = pieces[0].shape[0]
    out_rows, cols = out_ref.shape[1:]

    @pl.when(g == 0)
    def _():
        for s, piece in enumerate(pieces):
            all_ref[s * rows : (s + 1) * rows, :] = piece[...]
        all_ref[CHUNKS * rows :, :] = jnp.zeros_like(all_ref[CHUNKS * rows :, :])

    i, first_slot = lax.div(ph, share), lax.rem(ph, share) * out_rows
    h = jnp.bitwise_xor(irrep_ref[i], g)
    start = jnp.minimum(pick(offsets_of(count_ref)[:-1], h) + first_slot, CHUNKS * rows)
    base = pl.multiple_of(lax.div(start, 8) * 8, 8)
    window = all_ref[pl.ds(base, out_rows + 8), :]
    window = pltpu.roll(window, lax.rem(out_rows + 8 - (start - base), out_rows + 8), 0)[:out_rows]
    lane = lax.broadcasted_iota(jnp.int32, (VIRT_CAP, IRREPS), 1)
    row_slot = lax.broadcasted_iota(jnp.int32, (VIRT_CAP, 1), 0)
    e_row = jnp.sum(jnp.where(lane == h, vir_t_ref[...], 0.0), axis=1, keepdims=True)
    mine = jnp.zeros((out_rows, 1), jnp.float32)
    for position in range(share):
        part = e_row[position * out_rows : (position + 1) * out_rows]
        mine = jnp.where(lax.rem(ph, share) == position, part, mine)
    e_row = occ_ref[i] - mine
    row_slot = first_slot + lax.broadcasted_iota(jnp.int32, (out_rows, VIRT_CAP), 0)
    col_slot = lax.broadcasted_iota(jnp.int32, (out_rows, VIRT_CAP), 1)
    row_live = row_slot < count_ref[h]
    per_device = cols // VIRT_CAP
    for b in range(per_device):
        j = pair * per_device + b
        col_irrep = jnp.bitwise_xor(irrep_ref[j], g)
        e_col = occ_ref[j] - vir_ref[pl.ds(col_irrep, 1), :]
        lanes = slice(b * VIRT_CAP, (b + 1) * VIRT_CAP)
        live = row_live & (col_slot < count_ref[col_irrep])
        out_ref[0, :, lanes] = jnp.where(live, window[:, lanes], 0.0) / (e_row + e_col)


def expand(occ_irrep, vir_count, occ_energy, vir_energy, pieces, out_rows, share):
    cols = pieces[0].shape[1]
    rows = VIRTUALS // CHUNKS
    smem = pl.BlockSpec(memory_space=pltpu.SMEM)

    def whole(array):
        return pl.BlockSpec(array.shape, lambda g: (0,) * array.ndim)

    vir_t = vir_energy.T
    return pl.pallas_call(
        functools.partial(expand_kernel, share),
        out_shape=jax.ShapeDtypeStruct((IRREPS, out_rows, cols), jnp.float32),
        grid=(IRREPS,),
        in_specs=[smem, smem, smem, whole(vir_energy), whole(vir_t)] + [whole(piece) for piece in pieces],
        out_specs=pl.BlockSpec((1, out_rows, cols), lambda g: (g, 0, 0)),
        scratch_shapes=[pltpu.VMEM((CHUNKS * rows + out_rows + 8, cols), jnp.float32)],
        compiler_params=pltpu.CompilerParams(vmem_limit_bytes=VMEM_LIMIT),
    )(occ_irrep, vir_count, occ_energy, vir_energy, vir_t, *pieces)


def on_device(t_cycle, w_cycle, occ_energy, vir_energy, occ_irrep, vir_count):
    n_pair = lax.axis_size("pair")
    n_ph = lax.axis_size("ph")
    group = n_pair // ROW_OCC
    share = n_ph // ROW_OCC
    out_rows = t_cycle.shape[1] * n_pair // n_ph

    def swap(array, bits):
        return lax.ppermute(array, "pair", [(d, d ^ bits) for d in range(n_pair)])

    parts = [t_cycle] + [swap(t_cycle, m) for m in range(1, group)]
    own = compact_rows(occ_irrep, vir_count, parts)
    w_hi, w_lo = split_weights(occ_irrep, vir_count, w_cycle)
    pieces = []
    for s in range(CHUNKS):
        a, b = own[2 * s], own[2 * s + 1]
        near_a, near_b = swap(a, group), swap(b, group)
        far_a, far_b = swap(a, 2 * group), swap(b, 2 * group)
        held = {0: (a, b), 1: (near_a, near_b), 2: (far_a, far_b)}
        held[3] = (swap(near_a, 2 * group), swap(far_b, group))
        rows = []
        for q in range(ROW_OCC):
            for c in range(group):
                rows += [array if c == 0 else swap(array, c) for array in held[q]]
        partial_value = product(occ_irrep, vir_count, s, rows, w_hi, w_lo, group)
        summed = lax.psum_scatter(partial_value, "ph", scatter_dimension=0, tiled=True)
        if share > 1:
            groups = [[i * share + p for p in range(share)] for i in range(ROW_OCC)]
            summed = lax.all_gather(summed, "ph", axis=0, tiled=True, axis_index_groups=groups)
        pieces.append(summed)
    return expand(occ_irrep, vir_count, occ_energy, vir_energy, pieces, out_rows, share)


def solution(mesh):
    return jax.shard_map(
        on_device,
        mesh=mesh,
        in_specs=(P(None, "pair", "ph"), P(None, "ph", "pair"), P(), P(), P(), P()),
        out_specs=P(None, "ph", "pair"),
        check_vma=False,
    )
```

```python
import functools

import jax
import jax.numpy as jnp
from jax import lax
from jax.experimental import pallas as pl
from jax.experimental.pallas import tpu as pltpu
from jax.sharding import PartitionSpec as P

IRREPS = 8
VIRT_CAP = 128
VIRTUALS = 640
ROW_OCC = 4
ROW_ALIGN = 16
VMEM_LIMIT = 56 * 1024 * 1024


def offsets_of(count_ref):
    offs = [jnp.int32(0)]
    for h in range(IRREPS):
        offs.append(offs[-1] + count_ref[h])
    return offs


def pick(values, index):
    result = values[0]
    for position in range(1, len(values)):
        result = jnp.where(index == position, values[position], result)
    return result


def split_kernel(irrep_ref, count_ref, w_ref, hi_ref, lo_ref):
    g = pl.program_id(0)
    tile = w_ref.shape[1]
    per_tile = tile // VIRT_CAP
    first = (lax.axis_index("ph") * pl.num_programs(1) + pl.program_id(1)) * per_tile
    slot = lax.broadcasted_iota(jnp.int32, (VIRT_CAP, w_ref.shape[2]), 0)
    for k in range(per_tile):
        live = slot < count_ref[jnp.bitwise_xor(irrep_ref[first + k], g)]
        rows = pl.ds(k * VIRT_CAP, VIRT_CAP)
        value = jnp.where(live, w_ref[0, rows, :], 0.0)
        high = value.astype(jnp.bfloat16)
        hi_ref[0, rows, :] = high
        lo_ref[0, rows, :] = (value - high.astype(jnp.float32)).astype(jnp.bfloat16)


def split_weights(occ_irrep, vir_count, w):
    irreps, pairs, cols = w.shape
    tile = min(pairs, 1024)
    spec = pl.BlockSpec((1, tile, cols), lambda g, p, *_: (g, p, 0))
    part = jax.ShapeDtypeStruct(w.shape, jnp.bfloat16)
    return pl.pallas_call(
        split_kernel,
        out_shape=(part, part),
        grid_spec=pltpu.PrefetchScalarGridSpec(
            num_scalar_prefetch=2, grid=(irreps, pairs // tile), in_specs=[spec], out_specs=[spec, spec]
        ),
        compiler_params=pltpu.CompilerParams(vmem_limit_bytes=VMEM_LIMIT),
        cost_estimate=pl.CostEstimate(flops=4 * w.size, bytes_accessed=8 * w.size, transcendentals=0),
    )(occ_irrep, vir_count, w)


def compact_kernel(group, irrep_ref, count_ref, *refs):
    parts, outs = refs[:group], refs[group:]
    me = lax.axis_index("pair")
    sub, i = lax.rem(me, group), lax.div(me, group)
    local = parts[0].shape[1]
    half = outs[0].shape[0]
    offs = offsets_of(count_ref)
    irrep = irrep_ref[i]
    for piece, out in enumerate(outs):
        start = (piece // 2) * (2 * half * group) + sub * (2 * half) + (piece % 2) * half

        @pl.loop(0, half, unroll=4)
        def _(r, out=out, start=start):
            v = start + r
            h, base = jnp.int32(0), jnp.int32(0)
            for m in range(1, IRREPS):
                past = offs[m] <= v
                h = jnp.where(past, m, h)
                base = jnp.where(past, offs[m], base)
            a = v - base
            g = jnp.bitwise_xor(irrep, h)
            owner, row = jnp.bitwise_xor(lax.div(a, local), sub), lax.rem(a, local)
            if group == 2:
                out[pl.ds(r, 1), :] = jnp.where(
                    owner == 0, parts[0][g, pl.ds(row, 1), :], parts[1][g, pl.ds(row, 1), :]
                )
            else:
                for m in range(group):

                    @pl.when(owner == m)
                    def _(m=m):
                        out[pl.ds(r, 1), :] = parts[m][g, pl.ds(row, 1), :]


def compact_rows(occ_irrep, vir_count, parts, chunks):
    group = len(parts)
    half = VIRTUALS // (chunks * group * 2)
    pairs = parts[0].shape[2]
    vmem = pl.BlockSpec(memory_space=pltpu.VMEM)
    smem = pl.BlockSpec(memory_space=pltpu.SMEM)
    return pl.pallas_call(
        functools.partial(compact_kernel, group),
        out_shape=[jax.ShapeDtypeStruct((half, pairs), jnp.float32)] * (2 * chunks),
        in_specs=[smem, smem] + [vmem] * group,
        out_specs=[vmem] * (2 * chunks),
        compiler_params=pltpu.CompilerParams(vmem_limit_bytes=VMEM_LIMIT),
    )(occ_irrep, vir_count, *parts)


def product_kernel(group, chunk, irrep_ref, count_ref, *refs):
    n_parts = 2 * group * ROW_OCC
    parts, (whi_ref, wlo_ref, out_ref, rows_ref, hi_ref, lo_ref) = refs[:n_parts], refs[n_parts:]
    i, h = pl.program_id(0), pl.program_id(1)
    me = lax.axis_index("pair")
    sub, mine = lax.rem(me, group), lax.div(me, group)
    half = parts[0].shape[0]
    rows = rows_ref.shape[0]

    @pl.when(h == 0)
    def _():
        for q in range(ROW_OCC):

            @pl.when(jnp.bitwise_xor(i, mine) == q)
            def _(q=q):
                for c in range(group):
                    at = jnp.bitwise_xor(sub, c) * (2 * half)
                    for side in range(2):
                        rows_ref[pl.ds(pl.multiple_of(at + side * half, 8), half), :] = parts[
                            (q * group + c) * 2 + side
                        ][...]

        value = rows_ref[...]
        high = value.astype(jnp.bfloat16)
        hi_ref[...] = high
        lo_ref[...] = (value - high.astype(jnp.float32)).astype(jnp.bfloat16)
        out_ref[...] = jnp.zeros_like(out_ref)

    offs = offsets_of(count_ref)
    low, top = pick(offs[:-1], h) - chunk * rows, pick(offs[1:], h) - chunk * rows

    @pl.when((low < rows) & (top > 0))
    def _():
        window = min(rows, VIRT_CAP + ROW_ALIGN)
        base = lax.div(jnp.maximum(low, 0), ROW_ALIGN) * ROW_ALIGN
        base = pl.multiple_of(jnp.minimum(base, rows - window), ROW_ALIGN)
        high, rest = hi_ref[pl.ds(base, window), :], lo_ref[pl.ds(base, window), :]
        both = jnp.concatenate([high, rest], axis=0)
        first = jnp.dot(both, whi_ref[0], preferred_element_type=jnp.float32)
        second = jnp.dot(high, wlo_ref[0], preferred_element_type=jnp.float32)
        total = first[:window] + (first[window:] + second)
        row = base + lax.broadcasted_iota(jnp.int32, total.shape, 0)
        spot = pl.ds(base, window)
        out_ref[0, spot, :] = jnp.where((row >= low) & (row < top), total, out_ref[0, spot, :])


def product(occ_irrep, vir_count, chunk, parts, w_hi, w_lo, group):
    rows = 2 * group * parts[0].shape[0]
    irreps, pairs, cols = w_hi.shape

    def block_of(i, h, irrep_ref, count_ref):
        offs = offsets_of(count_ref)
        first, last = jnp.int32(0), jnp.int32(-1)
        for m in range(IRREPS):
            first = first + jnp.where(offs[m + 1] <= chunk * rows, 1, 0)
            last = last + jnp.where(offs[m] < (chunk + 1) * rows, 1, 0)
        return jnp.bitwise_xor(irrep_ref[i], jnp.clip(h, first, last)), 0, 0

    t_spec = pl.BlockSpec(parts[0].shape, lambda i, h, *_: (0, 0), pipeline_mode=pl.Buffered(1))
    w_spec = pl.BlockSpec((1, pairs, cols), block_of)
    out = pl.pallas_call(
        functools.partial(product_kernel, group, chunk),
        out_shape=jax.ShapeDtypeStruct((ROW_OCC, rows, cols), jnp.float32),
        grid_spec=pltpu.PrefetchScalarGridSpec(
            num_scalar_prefetch=2,
            grid=(ROW_OCC, irreps),
            in_specs=[t_spec] * len(parts) + [w_spec, w_spec],
            out_specs=pl.BlockSpec((1, rows, cols), lambda i, h, *_: (i, 0, 0)),
            scratch_shapes=[pltpu.VMEM((rows, pairs), dtype) for dtype in (jnp.float32, jnp.bfloat16, jnp.bfloat16)],
        ),
        compiler_params=pltpu.CompilerParams(vmem_limit_bytes=VMEM_LIMIT),
        cost_estimate=pl.CostEstimate(
            flops=2 * 6 * 2 * ROW_OCC * rows * pairs * cols, bytes_accessed=40 * 2**20, transcendentals=0
        ),
    )(occ_irrep, vir_count, *parts, w_hi, w_lo)
    return out.reshape(ROW_OCC * rows, cols)


def expand_kernel(share, irrep_ref, count_ref, occ_ref, vir_ref, vir_t_ref, *refs):
    pieces, (out_ref, all_ref) = refs[:-2], refs[-2:]
    g = pl.program_id(0)
    ph, pair = lax.axis_index("ph"), lax.axis_index("pair")
    rows = pieces[0].shape[0]
    out_rows, cols = out_ref.shape[1:]

    @pl.when(g == 0)
    def _():
        for s, piece in enumerate(pieces):
            all_ref[s * rows : (s + 1) * rows, :] = piece[...]
        all_ref[VIRTUALS:, :] = jnp.zeros_like(all_ref[VIRTUALS:, :])

    i, first_slot = lax.div(ph, share), lax.rem(ph, share) * out_rows
    h = jnp.bitwise_xor(irrep_ref[i], g)
    start = jnp.minimum(pick(offsets_of(count_ref)[:-1], h) + first_slot, VIRTUALS)
    base = pl.multiple_of(lax.div(start, 8) * 8, 8)
    window = all_ref[pl.ds(base, out_rows + 8), :]
    window = pltpu.roll(window, lax.rem(out_rows + 8 - (start - base), out_rows + 8), 0)[:out_rows]
    lane = lax.broadcasted_iota(jnp.int32, (VIRT_CAP, IRREPS), 1)
    row_slot = lax.broadcasted_iota(jnp.int32, (VIRT_CAP, 1), 0)
    e_row = jnp.sum(jnp.where(lane == h, vir_t_ref[...], 0.0), axis=1, keepdims=True)
    mine = jnp.zeros((out_rows, 1), jnp.float32)
    for position in range(share):
        part = e_row[position * out_rows : (position + 1) * out_rows]
        mine = jnp.where(lax.rem(ph, share) == position, part, mine)
    e_row = occ_ref[i] - mine
    row_slot = first_slot + lax.broadcasted_iota(jnp.int32, (out_rows, VIRT_CAP), 0)
    col_slot = lax.broadcasted_iota(jnp.int32, (out_rows, VIRT_CAP), 1)
    row_live = row_slot < count_ref[h]
    per_device = cols // VIRT_CAP
    for b in range(per_device):
        j = pair * per_device + b
        col_irrep = jnp.bitwise_xor(irrep_ref[j], g)
        e_col = occ_ref[j] - vir_ref[pl.ds(col_irrep, 1), :]
        lanes = slice(b * VIRT_CAP, (b + 1) * VIRT_CAP)
        live = row_live & (col_slot < count_ref[col_irrep])
        out_ref[0, :, lanes] = jnp.where(live, window[:, lanes], 0.0) / (e_row + e_col)


def expand(occ_irrep, vir_count, occ_energy, vir_energy, pieces, out_rows, share):
    cols = pieces[0].shape[1]
    smem = pl.BlockSpec(memory_space=pltpu.SMEM)

    def whole(array):
        return pl.BlockSpec(array.shape, lambda g: (0,) * array.ndim)

    vir_t = vir_energy.T
    return pl.pallas_call(
        functools.partial(expand_kernel, share),
        out_shape=jax.ShapeDtypeStruct((IRREPS, out_rows, cols), jnp.float32),
        grid=(IRREPS,),
        in_specs=[smem, smem, smem, whole(vir_energy), whole(vir_t)] + [whole(piece) for piece in pieces],
        out_specs=pl.BlockSpec((1, out_rows, cols), lambda g: (g, 0, 0)),
        scratch_shapes=[pltpu.VMEM((VIRTUALS + out_rows + 8, cols), jnp.float32)],
        compiler_params=pltpu.CompilerParams(vmem_limit_bytes=VMEM_LIMIT),
    )(occ_irrep, vir_count, occ_energy, vir_energy, vir_t, *pieces)


def on_device(t_cycle, w_cycle, occ_energy, vir_energy, occ_irrep, vir_count):
    n_pair = lax.axis_size("pair")
    n_ph = lax.axis_size("ph")
    group = n_pair // ROW_OCC
    share = n_ph // ROW_OCC
    out_rows = t_cycle.shape[1] * n_pair // n_ph

    def swap(array, bits):
        return lax.ppermute(array, "pair", [(d, d ^ bits) for d in range(n_pair)])

    parts = [t_cycle] + [swap(t_cycle, m) for m in range(1, group)]
    chunks = next(n for n in (2, 5, 1) if VIRTUALS % (16 * n * group) == 0)
    own = compact_rows(occ_irrep, vir_count, parts, chunks)
    w_hi, w_lo = split_weights(occ_irrep, vir_count, w_cycle)
    pieces = []
    for s in range(chunks):
        a, b = own[2 * s], own[2 * s + 1]
        near_a, near_b = swap(a, group), swap(b, group)
        far_a, far_b = swap(a, 2 * group), swap(b, 2 * group)
        held = {0: (a, b), 1: (near_a, near_b), 2: (far_a, far_b)}
        held[3] = (swap(near_a, 2 * group), swap(far_b, group))
        rows = []
        for q in range(ROW_OCC):
            for c in range(group):
                rows += [array if c == 0 else swap(array, c) for array in held[q]]
        partial_value = product(occ_irrep, vir_count, s, rows, w_hi, w_lo, group)
        summed = lax.psum_scatter(partial_value, "ph", scatter_dimension=0, tiled=True)
        if share > 1:
            groups = [[i * share + p for p in range(share)] for i in range(ROW_OCC)]
            summed = lax.all_gather(summed, "ph", axis=0, tiled=True, axis_index_groups=groups)
        pieces.append(summed)
    return expand(occ_irrep, vir_count, occ_energy, vir_energy, pieces, out_rows, share)


def solution(mesh):
    return jax.shard_map(
        on_device,
        mesh=mesh,
        in_specs=(P(None, "pair", "ph"), P(None, "ph", "pair"), P(), P(), P(), P()),
        out_specs=P(None, "ph", "pair"),
        check_vma=False,
    )
```

```python
import functools

import jax
import jax.numpy as jnp
from jax import lax
from jax.experimental import pallas as pl
from jax.experimental.pallas import tpu as pltpu
from jax.sharding import PartitionSpec as P

IRREPS = 8
VIRT_CAP = 128
VIRTUALS = 640
ROW_OCC = 4
ROW_ALIGN = 16
VMEM_LIMIT = 56 * 1024 * 1024


def offsets_of(count_ref):
    offs = [jnp.int32(0)]
    for h in range(IRREPS):
        offs.append(offs[-1] + count_ref[h])
    return offs


def pick(values, index):
    result = values[0]
    for position in range(1, len(values)):
        result = jnp.where(index == position, values[position], result)
    return result


def split_kernel(irrep_ref, count_ref, w_ref, hi_ref, lo_ref):
    g = pl.program_id(0)
    tile = w_ref.shape[1]
    per_tile = tile // VIRT_CAP
    first = (lax.axis_index("ph") * pl.num_programs(1) + pl.program_id(1)) * per_tile
    slot = lax.broadcasted_iota(jnp.int32, (VIRT_CAP, w_ref.shape[2]), 0)
    for k in range(per_tile):
        live = slot < count_ref[jnp.bitwise_xor(irrep_ref[first + k], g)]
        rows = pl.ds(k * VIRT_CAP, VIRT_CAP)
        value = jnp.where(live, w_ref[0, rows, :], 0.0)
        high = value.astype(jnp.bfloat16)
        hi_ref[0, rows, :] = high
        lo_ref[0, rows, :] = (value - high.astype(jnp.float32)).astype(jnp.bfloat16)


def split_weights(occ_irrep, vir_count, w):
    irreps, pairs, cols = w.shape
    tile = min(pairs, 1024)
    spec = pl.BlockSpec((1, tile, cols), lambda g, p, *_: (g, p, 0))
    part = jax.ShapeDtypeStruct(w.shape, jnp.bfloat16)
    return pl.pallas_call(
        split_kernel,
        out_shape=(part, part),
        grid_spec=pltpu.PrefetchScalarGridSpec(
            num_scalar_prefetch=2, grid=(irreps, pairs // tile), in_specs=[spec], out_specs=[spec, spec]
        ),
        compiler_params=pltpu.CompilerParams(vmem_limit_bytes=VMEM_LIMIT),
        cost_estimate=pl.CostEstimate(flops=4 * w.size, bytes_accessed=8 * w.size, transcendentals=0),
    )(occ_irrep, vir_count, w)


def compact_kernel(group, irrep_ref, count_ref, *refs):
    parts, outs = refs[:group], refs[group:]
    me = lax.axis_index("pair")
    sub, i = lax.rem(me, group), lax.div(me, group)
    local = parts[0].shape[1]
    half = outs[0].shape[0]
    offs = offsets_of(count_ref)
    irrep = irrep_ref[i]
    for piece, out in enumerate(outs):
        start = (piece // 2) * (2 * half * group) + sub * (2 * half) + (piece % 2) * half

        @pl.loop(0, half, unroll=4)
        def _(r, out=out, start=start):
            v = start + r
            h, base = jnp.int32(0), jnp.int32(0)
            for m in range(1, IRREPS):
                past = offs[m] <= v
                h = jnp.where(past, m, h)
                base = jnp.where(past, offs[m], base)
            a = v - base
            g = jnp.bitwise_xor(irrep, h)
            owner, row = jnp.bitwise_xor(lax.div(a, local), sub), lax.rem(a, local)
            if group == 2:
                out[pl.ds(r, 1), :] = jnp.where(
                    owner == 0, parts[0][g, pl.ds(row, 1), :], parts[1][g, pl.ds(row, 1), :]
                )
            else:
                for m in range(group):

                    @pl.when(owner == m)
                    def _(m=m):
                        out[pl.ds(r, 1), :] = parts[m][g, pl.ds(row, 1), :]


def compact_rows(occ_irrep, vir_count, parts, chunks):
    group = len(parts)
    half = VIRTUALS // (chunks * group * 2)
    pairs = parts[0].shape[2]
    vmem = pl.BlockSpec(memory_space=pltpu.VMEM)
    smem = pl.BlockSpec(memory_space=pltpu.SMEM)
    return pl.pallas_call(
        functools.partial(compact_kernel, group),
        out_shape=[jax.ShapeDtypeStruct((half, pairs), jnp.float32)] * (2 * chunks),
        in_specs=[smem, smem] + [vmem] * group,
        out_specs=[vmem] * (2 * chunks),
        compiler_params=pltpu.CompilerParams(vmem_limit_bytes=VMEM_LIMIT),
    )(occ_irrep, vir_count, *parts)


def product_kernel(group, chunk, irrep_ref, count_ref, *refs):
    n_parts = 2 * group * ROW_OCC
    parts, (whi_ref, wlo_ref, out_ref, rows_ref, hi_ref, lo_ref) = refs[:n_parts], refs[n_parts:]
    i, h = pl.program_id(0), pl.program_id(1)
    me = lax.axis_index("pair")
    sub, mine = lax.rem(me, group), lax.div(me, group)
    half = parts[0].shape[0]
    rows = rows_ref.shape[0]

    @pl.when(h == 0)
    def _():
        for q in range(ROW_OCC):

            @pl.when(jnp.bitwise_xor(i, mine) == q)
            def _(q=q):
                for c in range(group):
                    at = jnp.bitwise_xor(sub, c) * (2 * half)
                    for side in range(2):
                        rows_ref[pl.ds(pl.multiple_of(at + side * half, 8), half), :] = parts[
                            (q * group + c) * 2 + side
                        ][...]

        value = rows_ref[...]
        high = value.astype(jnp.bfloat16)
        hi_ref[...] = high
        lo_ref[...] = (value - high.astype(jnp.float32)).astype(jnp.bfloat16)
        out_ref[...] = jnp.zeros_like(out_ref)

    offs = offsets_of(count_ref)
    low, top = pick(offs[:-1], h) - chunk * rows, pick(offs[1:], h) - chunk * rows

    @pl.when((low < rows) & (top > 0))
    def _():
        window = min(rows, VIRT_CAP + ROW_ALIGN)
        base = lax.div(jnp.maximum(low, 0), ROW_ALIGN) * ROW_ALIGN
        base = pl.multiple_of(jnp.minimum(base, rows - window), ROW_ALIGN)
        high, rest = hi_ref[pl.ds(base, window), :], lo_ref[pl.ds(base, window), :]
        both = jnp.concatenate([high, rest], axis=0)
        first = jnp.dot(both, whi_ref[0], preferred_element_type=jnp.float32)
        second = jnp.dot(high, wlo_ref[0], preferred_element_type=jnp.float32)
        total = first[:window] + (first[window:] + second)
        row = base + lax.broadcasted_iota(jnp.int32, total.shape, 0)
        spot = pl.ds(base, window)
        out_ref[0, spot, :] = jnp.where((row >= low) & (row < top), total, out_ref[0, spot, :])


def product(occ_irrep, vir_count, chunk, parts, w_hi, w_lo, group):
    rows = 2 * group * parts[0].shape[0]
    irreps, pairs, cols = w_hi.shape

    def block_of(i, h, irrep_ref, count_ref):
        offs = offsets_of(count_ref)
        first, last = jnp.int32(0), jnp.int32(-1)
        for m in range(IRREPS):
            first = first + jnp.where(offs[m + 1] <= chunk * rows, 1, 0)
            last = last + jnp.where(offs[m] < (chunk + 1) * rows, 1, 0)
        return jnp.bitwise_xor(irrep_ref[i], jnp.clip(h, first, last)), 0, 0

    t_spec = pl.BlockSpec(parts[0].shape, lambda i, h, *_: (0, 0), pipeline_mode=pl.Buffered(1))
    w_spec = pl.BlockSpec((1, pairs, cols), block_of)
    out = pl.pallas_call(
        functools.partial(product_kernel, group, chunk),
        out_shape=jax.ShapeDtypeStruct((ROW_OCC, rows, cols), jnp.float32),
        grid_spec=pltpu.PrefetchScalarGridSpec(
            num_scalar_prefetch=2,
            grid=(ROW_OCC, irreps),
            in_specs=[t_spec] * len(parts) + [w_spec, w_spec],
            out_specs=pl.BlockSpec((1, rows, cols), lambda i, h, *_: (i, 0, 0)),
            scratch_shapes=[pltpu.VMEM((rows, pairs), dtype) for dtype in (jnp.float32, jnp.bfloat16, jnp.bfloat16)],
        ),
        compiler_params=pltpu.CompilerParams(vmem_limit_bytes=VMEM_LIMIT),
        cost_estimate=pl.CostEstimate(
            flops=2 * 6 * 2 * ROW_OCC * rows * pairs * cols, bytes_accessed=40 * 2**20, transcendentals=0
        ),
    )(occ_irrep, vir_count, *parts, w_hi, w_lo)
    return out.reshape(ROW_OCC * rows, cols)


def expand_kernel(share, irrep_ref, count_ref, occ_ref, vir_ref, vir_t_ref, *refs):
    pieces, (out_ref, all_ref) = refs[:-2], refs[-2:]
    g = pl.program_id(0)
    ph, pair = lax.axis_index("ph"), lax.axis_index("pair")
    rows = pieces[0].shape[0]
    out_rows, cols = out_ref.shape[1:]

    @pl.when(g == 0)
    def _():
        for s, piece in enumerate(pieces):
            all_ref[s * rows : (s + 1) * rows, :] = piece[...]
        all_ref[VIRTUALS:, :] = jnp.zeros_like(all_ref[VIRTUALS:, :])

    i, first_slot = lax.div(ph, share), lax.rem(ph, share) * out_rows
    h = jnp.bitwise_xor(irrep_ref[i], g)
    start = jnp.minimum(pick(offsets_of(count_ref)[:-1], h) + first_slot, VIRTUALS)
    base = pl.multiple_of(lax.div(start, 8) * 8, 8)
    window = all_ref[pl.ds(base, out_rows + 8), :]
    window = pltpu.roll(window, lax.rem(out_rows + 8 - (start - base), out_rows + 8), 0)[:out_rows]
    lane = lax.broadcasted_iota(jnp.int32, (VIRT_CAP, IRREPS), 1)
    row_slot = lax.broadcasted_iota(jnp.int32, (VIRT_CAP, 1), 0)
    e_row = jnp.sum(jnp.where(lane == h, vir_t_ref[...], 0.0), axis=1, keepdims=True)
    mine = jnp.zeros((out_rows, 1), jnp.float32)
    for position in range(share):
        part = e_row[position * out_rows : (position + 1) * out_rows]
        mine = jnp.where(lax.rem(ph, share) == position, part, mine)
    e_row = occ_ref[i] - mine
    row_slot = first_slot + lax.broadcasted_iota(jnp.int32, (out_rows, VIRT_CAP), 0)
    col_slot = lax.broadcasted_iota(jnp.int32, (out_rows, VIRT_CAP), 1)
    row_live = row_slot < count_ref[h]
    per_device = cols // VIRT_CAP
    for b in range(per_device):
        j = pair * per_device + b
        col_irrep = jnp.bitwise_xor(irrep_ref[j], g)
        e_col = occ_ref[j] - vir_ref[pl.ds(col_irrep, 1), :]
        lanes = slice(b * VIRT_CAP, (b + 1) * VIRT_CAP)
        live = row_live & (col_slot < count_ref[col_irrep])
        out_ref[0, :, lanes] = jnp.where(live, window[:, lanes], 0.0) / (e_row + e_col)


def expand(occ_irrep, vir_count, occ_energy, vir_energy, pieces, out_rows, share):
    cols = pieces[0].shape[1]
    smem = pl.BlockSpec(memory_space=pltpu.SMEM)

    def whole(array):
        return pl.BlockSpec(array.shape, lambda g: (0,) * array.ndim)

    vir_t = vir_energy.T
    return pl.pallas_call(
        functools.partial(expand_kernel, share),
        out_shape=jax.ShapeDtypeStruct((IRREPS, out_rows, cols), jnp.float32),
        grid=(IRREPS,),
        in_specs=[smem, smem, smem, whole(vir_energy), whole(vir_t)] + [whole(piece) for piece in pieces],
        out_specs=pl.BlockSpec((1, out_rows, cols), lambda g: (g, 0, 0)),
        scratch_shapes=[pltpu.VMEM((VIRTUALS + out_rows + 8, cols), jnp.float32)],
        compiler_params=pltpu.CompilerParams(vmem_limit_bytes=VMEM_LIMIT),
    )(occ_irrep, vir_count, occ_energy, vir_energy, vir_t, *pieces)


def after_kernel(array_ref, other_ref, out_ref):
    pass


def after(array, other):
    anywhere = pl.BlockSpec(memory_space=pl.ANY)
    return pl.pallas_call(
        after_kernel,
        out_shape=jax.ShapeDtypeStruct(array.shape, array.dtype),
        in_specs=[anywhere, anywhere],
        out_specs=anywhere,
        input_output_aliases={0: 0},
        cost_estimate=pl.CostEstimate(flops=0, bytes_accessed=0, transcendentals=0),
    )(array, other)


def on_device(t_cycle, w_cycle, occ_energy, vir_energy, occ_irrep, vir_count):
    n_pair = lax.axis_size("pair")
    n_ph = lax.axis_size("ph")
    group = n_pair // ROW_OCC
    share = n_ph // ROW_OCC
    out_rows = t_cycle.shape[1] * n_pair // n_ph

    def swap(array, bits):
        return lax.ppermute(array, "pair", [(d, d ^ bits) for d in range(n_pair)])

    parts = [t_cycle] + [swap(t_cycle, m) for m in range(1, group)]
    chunks = next(n for n in (2, 5, 1) if VIRTUALS % (16 * n * group) == 0)
    own = compact_rows(occ_irrep, vir_count, parts, chunks)
    w_hi, w_lo = split_weights(occ_irrep, vir_count, w_cycle)
    pieces = []
    earlier = w_hi
    for s in range(chunks):
        a, b = own[2 * s], own[2 * s + 1]
        near_a, near_b = swap(a, group), swap(b, group)
        far_a, far_b = swap(a, 2 * group), swap(b, 2 * group)
        near_a, far_b = after(near_a, earlier), after(far_b, earlier)
        held = {0: (a, b), 1: (near_a, near_b), 2: (far_a, far_b)}
        held[3] = (swap(near_a, 2 * group), swap(far_b, group))
        rows = []
        for q in range(ROW_OCC):
            for c in range(group):
                rows += [array if c == 0 else swap(array, c) for array in held[q]]
        partial_value = product(occ_irrep, vir_count, s, rows, w_hi, w_lo, group)
        earlier = partial_value
        summed = lax.psum_scatter(partial_value, "ph", scatter_dimension=0, tiled=True)
        if share > 1:
            groups = [[i * share + p for p in range(share)] for i in range(ROW_OCC)]
            summed = lax.all_gather(summed, "ph", axis=0, tiled=True, axis_index_groups=groups)
        pieces.append(summed)
    return expand(occ_irrep, vir_count, occ_energy, vir_energy, pieces, out_rows, share)


def solution(mesh):
    return jax.shard_map(
        on_device,
        mesh=mesh,
        in_specs=(P(None, "pair", "ph"), P(None, "ph", "pair"), P(), P(), P(), P()),
        out_specs=P(None, "ph", "pair"),
        check_vma=False,
    )
```
